32 devices in a mesh: expert: 16 (over z, y, x), mp: 2 (over core).
Axes of the slice: x: 2, y: 2, z: 4, core: 2. Of those that a mesh axis runs over, the one named last changes fastest.
Arguments:
- partials: bfloat16 [16, 2, 1024, 768], P('expert', None, None, 'mp'), may hold values from -6 to 6
- counts: int32 [8], replicated, may hold values from 1 to 8, as said below
- slot_expert: int32 [16], replicated, may hold values from 0 to 7, as said below
- owner: int32 [16], replicated, may hold values from 0 to 15, each once
- left: float32 [16, 1024, 1024], P('expert', 'mp')
- right: float32 [16, 768, 768], P('expert', 'mp')
- left_root: bfloat16 [16, 1024, 1024], P('expert'), as said below
- right_root: bfloat16 [16, 768, 768], P('expert', 'mp'), as said below
Outputs:
- update: bfloat16 [16, 2, 1024, 768], P('expert', None, None, 'mp')
- left_next: float32 [16, 1024, 1024], P('expert', 'mp')
- right_next: float32 [16, 768, 768], P('expert', 'mp')
The draws below stay inside these ranges and needn't reach their ends.
Inputs may be any that keep to these rules, and one draw needn't show every extreme that they name: counts[e] is the number of entries of slot_expert equal to e; they sum to 16 and one expert has exactly 8. `slot_expert`: every expert is named by some entry. `owner`: each device owns exactly one block. `left_root`: each matrix is symmetric. `right_root`: each matrix is symmetric.
All inputs are finite; a program needn't handle non-finite values.
Results may differ from the reference program's by a relative error of at most 0.0052.
Values may be sent and summed in bfloat16 or wider, within the bound.
A program may use at most 64 MiB of HBM per device.

```python
import math
import jax
import jax.numpy as jnp
from jax import lax

SPLIT = 2
BR = 1024
NC = 768
MAXREP = 8
BLOCKS = 16
EXPERTS = 8
REPLICAS = 16


def replica_layout(key):
    order_key = jax.random.fold_in(key, 5)
    slot_key = jax.random.fold_in(key, 7)
    ranking = jax.random.permutation(order_key, EXPERTS)
    labels = jnp.arange(EXPERTS, dtype=jnp.int32)
    ranks = jnp.zeros((EXPERTS,), jnp.int32).at[ranking].set(labels)
    counts = jnp.where(ranks == 0, MAXREP, jnp.where(ranks <= EXPERTS - MAXREP + 1, 2, 1)).astype(jnp.int32)
    ends = jnp.cumsum(counts)
    slots = jnp.arange(REPLICAS, dtype=jnp.int32)
    expert_of = jnp.sum((slots[:, None] >= ends[None, :]).astype(jnp.int32), axis=1)
    shuffle = jax.random.permutation(slot_key, REPLICAS)
    return (counts, expert_of[shuffle].astype(jnp.int32))


def draw_counts(key, part):
    counts, placed = replica_layout(key)
    return counts


def draw_slot_expert(key, part):
    counts, placed = replica_layout(key)
    return placed


def shaped(noise, key, width, low, high, spread):
    mixed = (noise + jnp.swapaxes(noise, 1, 2)) * (spread / math.sqrt(2.0 * width))
    diagonal = jnp.exp(jax.random.uniform(key, noise.shape[:2], jnp.float32, math.log(low), math.log(high)))
    identity = (lax.broadcasted_iota(jnp.int32, (width, width), 0) == lax.broadcasted_iota(jnp.int32, (width, width), 1)).astype(jnp.float32)
    return mixed + identity[None, :, :] * diagonal[:, None, :]


def draw_left(key, part):
    key = jax.random.fold_in(key, 11)
    first, second = jax.random.split(key)
    noise = jax.random.normal(first, (BLOCKS, BR, BR), jnp.float32)
    return shaped(noise, second, BR, 0.8, 2.5, 0.3)


def draw_right(key, part):
    key = jax.random.fold_in(key, 13)
    first, second = jax.random.split(key)
    noise = jax.random.normal(first, (BLOCKS, NC, NC), jnp.float32)
    return shaped(noise, second, NC, 0.8, 2.5, 0.3)


def draw_left_root(key, part):
    key = jax.random.fold_in(key, 17)
    first, second = jax.random.split(key)
    noise = jax.random.normal(first, (BLOCKS, BR, BR), jnp.float32)
    return shaped(noise, second, BR, 0.8, 2.5, 0.3).astype(jnp.bfloat16)


def draw_right_root(key, part):
    key = jax.random.fold_in(key, 19)
    first, second = jax.random.split(key)
    noise = jax.random.normal(first, (BLOCKS, NC, NC), jnp.float32)
    return shaped(noise, second, NC, 0.8, 2.5, 0.3).astype(jnp.bfloat16)


def steps_of(own_key, dims, shards, least, largest):
    factor_of = 1.0
    for dim, shards_of in shards:
        steps = jax.random.uniform(jax.random.fold_in(jax.random.fold_in(own_key, 6), dim), (shards_of,), jnp.float32, least / len(shards), largest / len(shards))
        factor_of = factor_of * jnp.repeat(jnp.exp(steps), dims[dim] // shards_of).reshape((-1,) + (1,) * (len(dims) - 1 - dim))
    return factor_of


def bell_draw(key, extent, scale, most, shards=(), held_as=jnp.bfloat16):
    gain = steps_of(key, extent, shards, -0.22, 0.18) if shards else 1.0
    values = jax.random.normal(key, extent, jnp.float32) * scale * gain
    return jnp.minimum(jnp.maximum(values, -most), most).astype(held_as)


def setup_inputs(seed: int = 0) -> dict:
    keys = jax.random.split(jax.random.key(seed), 9)
    partials = bell_draw(keys[0], (REPLICAS, SPLIT, BR, NC), 1.0, 6.0, ((0, 16), (3, 2)))
    counts = draw_counts(jax.random.fold_in(keys[8], 71), 0)
    slot_expert = draw_slot_expert(jax.random.fold_in(keys[8], 71), 0)
    owner = jax.random.permutation(keys[3], BLOCKS).astype(jnp.int32)
    left = draw_left(jax.random.fold_in(keys[8], 71), 0)
    right = draw_right(jax.random.fold_in(keys[8], 71), 0)
    left_root = draw_left_root(jax.random.fold_in(keys[8], 71), 0)
    right_root = draw_right_root(jax.random.fold_in(keys[8], 71), 0)
    return dict(partials=partials, counts=counts, slot_expert=slot_expert, owner=owner, left=left, right=right, left_root=left_root, right_root=right_root)


def reference(partials, counts, slot_expert, owner, left, right, left_root, right_root):
    experts = counts.shape[0]
    blocks = owner.shape[0]
    row_count = partials.shape[2]
    col_count = partials.shape[3]

    def add_slot(summed, slot_index):
        slot_grad = partials[slot_index].astype(jnp.float32)
        return summed.at[slot_expert[slot_index]].add(slot_grad), None

    start = jnp.zeros((experts, SPLIT, row_count, col_count), jnp.float32)
    summed, unused = lax.scan(add_slot, start, jnp.arange(partials.shape[0], dtype=jnp.int32))
    averaged = (summed / counts.astype(jnp.float32)[:, None, None, None]).astype(jnp.bfloat16)
    grad_blocks = averaged.reshape(experts * SPLIT, row_count, col_count)
    positions = jnp.arange(blocks, dtype=jnp.int32)
    inverse = jnp.zeros((blocks,), jnp.int32).at[owner].set(positions)

    def per_owner(owner_index):
        current = grad_blocks[inverse[owner_index]]
        left_new = left[owner_index] + jnp.dot(current, current.T, preferred_element_type=jnp.float32) / col_count
        right_new = right[owner_index] + jnp.dot(current.T, current, preferred_element_type=jnp.float32) / row_count
        middle = jnp.dot(current, right_root[owner_index], preferred_element_type=jnp.float32).astype(jnp.bfloat16)
        precond = jnp.dot(left_root[owner_index], middle, preferred_element_type=jnp.float32).astype(jnp.bfloat16)
        return left_new, right_new, precond

    left_next, right_next, precond = lax.map(per_owner, positions)
    by_block = precond[owner].reshape(experts, SPLIT, row_count, col_count)
    update = by_block[slot_expert]
    return update, left_next, right_next
```

```python
import functools

import jax
import jax.numpy as jnp
from jax import lax
from jax.experimental import pallas as pl
from jax.experimental.pallas import tpu as pltpu
from jax.sharding import PartitionSpec as P

GROUPS = 2
CHUNKS = 4
AHEAD = 2


def kernel(
    n, groups, chunks, table, partials, left, right, left_root, right_root,
    update, left_next, right_next,
    arrived, running, sums, blocks, grad, middle, precond, spread, picked,
    left_buf, right_buf, lroot_buf, rroot_buf,
    load_sem, send_a, recv_a, send_b, recv_b, send_p, recv_p, send_c, recv_c, send_d, recv_d, store_sem,
):
    size = n // groups
    halves, rows, cols = partials.shape[1:]
    part = rows // chunks
    sub = part // size
    full_cols = grad.shape[1]
    me = lax.axis_index("expert")
    core = lax.axis_index("mp")
    first = me // size * size
    place = lax.rem(me, size)
    keep_at, source_at, half_at = size, 2 * size, 2 * size + n
    fetch_at, count_at = 2 * size + 2 * n, 2 * size + 2 * n + halves * size

    def remote(src, dst, send, recv, peer):
        return pltpu.make_async_remote_copy(
            src_ref=src, dst_ref=dst, send_sem=send, recv_sem=recv,
            device_id=peer, device_id_type=pl.DeviceIdType.MESH,
        )

    def wait_bytes(ref, sem):
        pltpu.make_async_copy(ref, ref, sem).wait()

    def row_slab(chunk, index):
        return pl.ds(pl.multiple_of(chunk * part + index * sub, sub), sub)

    my_cols = pl.ds(pl.multiple_of(core * cols, 128), cols)

    loads = [
        pltpu.make_async_copy(right_root.at[0], rroot_buf, load_sem.at[0]),
        pltpu.make_async_copy(left_root.at[0], lroot_buf, load_sem.at[1]),
        pltpu.make_async_copy(left.at[0], left_buf, load_sem.at[2]),
        pltpu.make_async_copy(right.at[0], right_buf, load_sem.at[3]),
    ]

    barrier = pltpu.get_barrier_semaphore()

    def greet(step, carry):
        pl.semaphore_signal(
            barrier, inc=1, device_id={"expert": lax.rem(me + step, n)},
            device_id_type=pl.DeviceIdType.MESH,
        )
        return carry

    lax.fori_loop(1, n, greet, 0)
    pl.semaphore_signal(barrier, inc=1, device_id={"mp": 1 - core}, device_id_type=pl.DeviceIdType.MESH)
    pl.semaphore_wait(barrier, n)

    def scatter_partials(chunk):
        def body(step, carry):
            index = lax.rem(place + step, size)
            remote(
                partials.at[0, :, row_slab(chunk, index), :],
                arrived[chunk].at[place], send_a.at[chunk], recv_a.at[chunk],
                {"expert": first + index},
            ).start()
            return carry

        lax.fori_loop(1, size, body, 0)
        pltpu.make_async_copy(
            partials.at[0, :, row_slab(chunk, place), :], arrived[chunk].at[place], recv_a.at[chunk]
        ).start()

    def send_sums(chunk):
        wait_bytes(arrived[chunk], recv_a.at[chunk])
        for half in range(halves):
            def add(rank, total):
                keep = table[keep_at + rank].astype(jnp.float32)
                total = total * keep + arrived[chunk][table[rank], half].astype(jnp.float32)
                running[rank, half] = total.astype(jnp.bfloat16)
                return total

            lax.fori_loop(0, size, add, jnp.zeros((sub, cols), jnp.float32))

        def send(step, carry):
            peer = lax.rem(me + step, n)
            sums[chunk, peer] = running[table[source_at + peer], table[half_at + peer]]
            remote(
                sums.at[chunk, peer], blocks.at[chunk, me], send_b.at[chunk], recv_b.at[chunk],
                {"expert": peer},
            ).start()
            return carry

        lax.fori_loop(1, n, send, 0)
        sums[chunk, me] = running[table[source_at + me], table[half_at + me]]
        pltpu.make_async_copy(sums.at[chunk, me], blocks.at[chunk, me], recv_b.at[chunk]).start()

    def form_grad(chunk):
        wait_bytes(blocks.at[chunk], recv_b.at[chunk])
        count = table[count_at].astype(jnp.float32)

        def form(index, carry):
            total = blocks[chunk, index].astype(jnp.float32)
            for group in range(1, groups):
                total = total + blocks[chunk, group * size + index].astype(jnp.float32)
            grad[row_slab(chunk, index), my_cols] = (total / count).astype(jnp.bfloat16)
            return carry

        lax.fori_loop(0, size, form, 0)
        swap(chunk).start()

    def swap(chunk):
        rows_of = pl.ds(chunk * part, part)
        return remote(
            grad.at[rows_of, my_cols], grad.at[rows_of, my_cols],
            send_p.at[chunk], recv_p.at[chunk], {"mp": 1 - core},
        )

    def form_middle(chunk):
        rows_of = pl.ds(chunk * part, part)
        swap(chunk).wait_recv()
        middle[rows_of, :] = lax.dot_general(
            grad[rows_of, :], rroot_buf[...], (((1,), (1,)), ((), ())), preferred_element_type=jnp.float32
        ).astype(jnp.bfloat16)

    def scatter_precond(chunk):
        rows_of = pl.ds(chunk * part, part)
        precond[rows_of, :] = jnp.dot(
            lroot_buf[rows_of, :], middle[...], preferred_element_type=jnp.float32
        ).astype(jnp.bfloat16)

        def body(step, carry):
            peer = lax.rem(me + step, n)
            remote(
                precond.at[row_slab(chunk, lax.rem(peer, size)), :], spread[chunk].at[me],
                send_c.at[chunk], recv_c.at[chunk], {"expert": peer},
            ).start()
            return carry

        lax.fori_loop(1, n, body, 0)
        pltpu.make_async_copy(
            precond.at[row_slab(chunk, place), :], spread[chunk].at[me], recv_c.at[chunk]
        ).start()

    def return_blocks(chunk):
        wait_bytes(spread[chunk], recv_c.at[chunk])

        def pick(index):
            for half in range(halves):
                picked[chunk, index, half] = spread[chunk][table[fetch_at + halves * index + half]]

        def body(step, carry):
            index = lax.rem(place + step, size)
            pick(index)
            remote(
                picked.at[chunk, index], update.at[0, :, row_slab(chunk, place), :],
                send_d.at[chunk], recv_d.at[chunk], {"expert": first + index},
            ).start()
            return carry

        lax.fori_loop(1, size, body, 0)
        pick(place)
        pltpu.make_async_copy(
            picked.at[chunk, place], update.at[0, :, row_slab(chunk, place), :], recv_d.at[chunk]
        ).start()

    for chunk in range(min(AHEAD, chunks)):
        scatter_partials(chunk)
    for load in loads:
        load.start()
    running[size] = jnp.zeros_like(running[size])
    loads[0].wait()
    for chunk in range(chunks):
        send_sums(chunk)
        if chunk + AHEAD < chunks:
            scatter_partials(chunk + AHEAD)
    for chunk in range(chunks):
        form_grad(chunk)
        if chunk:
            form_middle(chunk - 1)
    form_middle(chunks - 1)
    loads[1].wait()
    for chunk in range(chunks):
        scatter_precond(chunk)

    half_rows = left_buf.shape[0]
    loads[2].wait()
    tile = 128

    def add_left(index, carry):
        rows_of = pl.ds(pl.multiple_of(index * tile, tile), tile)
        product = lax.dot_general(
            grad[pl.ds(pl.multiple_of(core * half_rows + index * tile, tile), tile), :], grad[...],
            (((1,), (1,)), ((), ())), preferred_element_type=jnp.float32,
        )
        left_buf[rows_of, :] = left_buf[rows_of, :] + product / full_cols
        return carry

    lax.fori_loop(0, half_rows // tile, add_left, 0)
    left_store = pltpu.make_async_copy(left_buf, left_next.at[0], store_sem.at[0])
    left_store.start()
    loads[3].wait()

    def add_right(index, carry):
        rows_of = pl.ds(pl.multiple_of(index * tile, tile), tile)
        product = lax.dot_general(
            grad[:, pl.ds(pl.multiple_of(core * cols + index * tile, tile), tile)], grad[...],
            (((0,), (0,)), ((), ())), preferred_element_type=jnp.float32,
        )
        right_buf[rows_of, :] = right_buf[rows_of, :] + product / rows
        return carry

    lax.fori_loop(0, cols // tile, add_right, 0)
    right_store = pltpu.make_async_copy(right_buf, right_next.at[0], store_sem.at[1])
    right_store.start()

    for chunk in range(chunks):
        return_blocks(chunk)
    left_store.wait()
    right_store.wait()
    for chunk in range(chunks):
        wait_bytes(arrived[chunk].at[pl.ds(0, size - 1)], send_a.at[chunk])
        wait_bytes(sums.at[chunk, pl.ds(0, n - 1)], send_b.at[chunk])
        swap(chunk).wait_send()
        wait_bytes(spread[chunk].at[pl.ds(0, n - 1)], send_c.at[chunk])
        wait_bytes(picked.at[chunk, pl.ds(0, size - 1)], send_d.at[chunk])
    for chunk in range(chunks):
        wait_bytes(update.at[0, :, pl.ds(chunk * part, part), :], recv_d.at[chunk])


def index_table(n, groups, halves, counts, slot_expert, owner):
    size = n // groups
    me = lax.axis_index("expert")
    experts = lax.dynamic_slice_in_dim(slot_expert, me // size * size, size)
    position = jnp.arange(size, dtype=jnp.int32)
    before = (experts[None, :] < experts[:, None]) | (
        (experts[None, :] == experts[:, None]) & (position[None, :] < position[:, None])
    )
    rank = jnp.sum(before, axis=1, dtype=jnp.int32)
    placed = rank[None, :] == position[:, None]
    order = jnp.sum(jnp.where(placed, position[None, :], 0), axis=1, dtype=jnp.int32)
    sorted_experts = jnp.sum(jnp.where(placed, experts[None, :], 0), axis=1, dtype=jnp.int32)
    previous = jnp.concatenate([jnp.full((1,), -1, jnp.int32), sorted_experts[:-1]])
    keep = (sorted_experts == previous).astype(jnp.int32)
    blocks = jnp.arange(n, dtype=jnp.int32)
    block_of = jnp.sum(jnp.where(owner[None, :] == blocks[:, None], blocks[None, :], 0), axis=1, dtype=jnp.int32)
    expert_of = block_of // halves
    same = experts[None, :] == expert_of[:, None]
    upto = jnp.sum(experts[None, :] <= expert_of[:, None], axis=1, dtype=jnp.int32)
    source = jnp.where(jnp.any(same, axis=1), upto - 1, size)
    wanted = (halves * experts[:, None] + jnp.arange(halves, dtype=jnp.int32)[None, :]).reshape(-1)
    fetch = jnp.sum(jnp.where(wanted[:, None] == blocks[None, :], owner[None, :], 0), axis=1, dtype=jnp.int32)
    mine = jnp.sum(jnp.where(blocks == me, expert_of, 0), dtype=jnp.int32)
    labels = jnp.arange(counts.shape[0], dtype=jnp.int32)
    count = jnp.sum(jnp.where(labels == mine, counts, 0), dtype=jnp.int32)
    return jnp.concatenate([order, keep, source, block_of % halves, fetch, count[None]])


def on_device(n, partials, counts, slot_expert, owner, left, right, left_root, right_root):
    halves, rows, cols = partials.shape[1:]
    groups = GROUPS
    size = n // groups
    chunks = max(1, min(CHUNKS, rows // (16 * size)))
    sub = rows // chunks // size
    full_cols = right.shape[2]
    table = index_table(n, groups, halves, counts, slot_expert, owner)
    anywhere = pl.BlockSpec(memory_space=pl.ANY)
    bf16 = jnp.bfloat16
    dma = pltpu.SemaphoreType.DMA
    update, left_next, right_next = pl.pallas_call(
        functools.partial(kernel, n, groups, chunks),
        out_shape=(
            jax.ShapeDtypeStruct(partials.shape, bf16),
            jax.ShapeDtypeStruct(left.shape, jnp.float32),
            jax.ShapeDtypeStruct(right.shape, jnp.float32),
        ),
        in_specs=[pl.BlockSpec(memory_space=pltpu.SMEM)] + [anywhere] * 5,
        out_specs=(anywhere,) * 3,
        scratch_shapes=[
            [pltpu.VMEM((size, halves, sub, cols), bf16)] * chunks,
            pltpu.VMEM((size + 1, halves, sub, cols), bf16),
            pltpu.VMEM((chunks, n, sub, cols), bf16),
            pltpu.VMEM((chunks, n, sub, cols), bf16),
            pltpu.VMEM((rows, full_cols), bf16),
            pltpu.VMEM((rows, cols), bf16),
            pltpu.VMEM((rows, cols), bf16),
            [pltpu.VMEM((n, sub, cols), bf16)] * chunks,
            pltpu.VMEM((chunks, size, halves, sub, cols), bf16),
            pltpu.VMEM(left.shape[1:], jnp.float32),
            pltpu.VMEM(right.shape[1:], jnp.float32),
            pltpu.VMEM(left_root.shape[1:], bf16),
            pltpu.VMEM(right_root.shape[1:], bf16),
            dma((4,)),
        ]
        + [dma((chunks,))] * 10
        + [dma((2,))],
        compiler_params=pltpu.CompilerParams(
            collective_id=0, has_side_effects=True, vmem_limit_bytes=48 * 1024 * 1024
        ),
    )(table, partials, left, right, left_root, right_root)
    return update, left_next, right_next


def solution(mesh):
    return jax.shard_map(
        functools.partial(on_device, mesh.shape["expert"]),
        mesh=mesh,
        in_specs=(
            P("expert", None, None, "mp"),
            P(),
            P(),
            P(),
            P("expert", "mp", None),
            P("expert", "mp", None),
            P("expert", None, None),
            P("expert", "mp", None),
        ),
        out_specs=(P("expert", None, None, "mp"), P("expert", "mp", None), P("expert", "mp", None)),
        check_vma=False,
    )
```

```python
import functools

import jax
import jax.numpy as jnp
from jax import lax
from jax.experimental import pallas as pl
from jax.experimental.pallas import tpu as pltpu
from jax.sharding import PartitionSpec as P

GROUPS = 2
CHUNKS = 4
AHEAD = 3


def kernel(
    n, groups, chunks, counts, slot_expert, owner, partials, left, right, left_root, right_root,
    update, left_next, right_next,
    table, arrived, running, sums, blocks, grad, middle, precond, spread, picked,
    left_buf, right_buf, lroot_buf, rroot_buf,
    load_sem, send_a, recv_a, send_b, recv_b, send_p, recv_p, send_c, recv_c, send_d, recv_d, store_sem,
):
    size = n // groups
    halves, rows, cols = partials.shape[1:]
    part = rows // chunks
    sub = part // size
    full_cols = grad.shape[1]
    me = lax.axis_index("expert")
    core = lax.axis_index("mp")
    first = me // size * size
    place = lax.rem(me, size)
    source_at, half_at = size, size + n

    def remote(src, dst, send, recv, peer):
        return pltpu.make_async_remote_copy(
            src_ref=src, dst_ref=dst, send_sem=send, recv_sem=recv,
            device_id=peer, device_id_type=pl.DeviceIdType.MESH,
        )

    def wait_bytes(ref, sem):
        pltpu.make_async_copy(ref, ref, sem).wait()

    def row_slab(chunk, index):
        return pl.ds(pl.multiple_of(chunk * part + index * sub, sub), sub)

    my_cols = pl.ds(pl.multiple_of(core * cols, 128), cols)

    loads = [
        pltpu.make_async_copy(right_root.at[0], rroot_buf, load_sem.at[0]),
        pltpu.make_async_copy(left_root.at[0], lroot_buf, load_sem.at[1]),
        pltpu.make_async_copy(left.at[0], left_buf, load_sem.at[2]),
        pltpu.make_async_copy(right.at[0], right_buf, load_sem.at[3]),
    ]

    barrier = pltpu.get_barrier_semaphore()

    def greet(step, carry):
        pl.semaphore_signal(
            barrier, inc=1, device_id={"expert": lax.rem(me + step, n)},
            device_id_type=pl.DeviceIdType.MESH,
        )
        return carry

    lax.fori_loop(1, n, greet, 0)
    pl.semaphore_signal(barrier, inc=1, device_id={"mp": 1 - core}, device_id_type=pl.DeviceIdType.MESH)
    pl.semaphore_wait(barrier, n)

    def scatter_partials(chunk):
        def body(step, carry):
            index = lax.rem(place + step, size)
            remote(
                partials.at[0, :, row_slab(chunk, index), :],
                arrived[chunk].at[place], send_a.at[chunk], recv_a.at[chunk],
                {"expert": first + index},
            ).start()
            return carry

        lax.fori_loop(1, size, body, 0)
        pltpu.make_async_copy(
            partials.at[0, :, row_slab(chunk, place), :], arrived[chunk].at[place], recv_a.at[chunk]
        ).start()

    def block_at(device):
        return lax.fori_loop(
            0, n, lambda block, found: jnp.where(owner[block] == device, block, found), jnp.int32(0), unroll=8
        )

    def fill_table():
        def link(index, carry):
            expert = slot_expert[first + index]
            table[index] = lax.fori_loop(
                0, size,
                lambda other, found: jnp.where(
                    (slot_expert[first + other] == expert) & (other < index), other, found
                ),
                jnp.int32(size), unroll=8,
            )
            return carry

        lax.fori_loop(0, size, link, 0)

        def locate(device, carry):
            block = block_at(device)
            expert = block // halves
            table[source_at + device] = lax.fori_loop(
                0, size,
                lambda other, found: jnp.where(slot_expert[first + other] == expert, other, found),
                jnp.int32(size), unroll=8,
            )
            table[half_at + device] = block - expert * halves
            return carry

        lax.fori_loop(0, n, locate, 0)

    def half_sum(device):
        return running[table[source_at + device], table[half_at + device]].astype(jnp.bfloat16)

    def send_sums(chunk):
        wait_bytes(arrived[chunk], recv_a.at[chunk])
        for half in range(halves):
            def add(index, carry):
                running[index, half] = running[table[index], half] + arrived[chunk][index, half].astype(jnp.float32)
                return carry

            lax.fori_loop(0, size, add, 0)

        def send(step, carry):
            peer = lax.rem(me + step, n)
            sums[chunk, peer] = half_sum(peer)
            remote(
                sums.at[chunk, peer], blocks.at[chunk, me], send_b.at[chunk], recv_b.at[chunk],
                {"expert": peer},
            ).start()
            return carry

        lax.fori_loop(1, n, send, 0)
        sums[chunk, me] = half_sum(me)
        pltpu.make_async_copy(sums.at[chunk, me], blocks.at[chunk, me], recv_b.at[chunk]).start()

    def form_grad(chunk):
        wait_bytes(blocks.at[chunk], recv_b.at[chunk])
        count = counts[block_at(me) // halves].astype(jnp.float32)

        def form(index, carry):
            total = blocks[chunk, index].astype(jnp.float32)
            for group in range(1, groups):
                total = total + blocks[chunk, group * size + index].astype(jnp.float32)
            grad[row_slab(chunk, index), my_cols] = (total / count).astype(jnp.bfloat16)
            return carry

        lax.fori_loop(0, size, form, 0)
        swap(chunk).start()

    def swap(chunk):
        rows_of = pl.ds(chunk * part, part)
        return remote(
            grad.at[rows_of, my_cols], grad.at[rows_of, my_cols],
            send_p.at[chunk], recv_p.at[chunk], {"mp": 1 - core},
        )

    def form_middle(chunk):
        rows_of = pl.ds(chunk * part, part)
        swap(chunk).wait_recv()
        middle[rows_of, :] = lax.dot_general(
            grad[rows_of, :], rroot_buf[...], (((1,), (1,)), ((), ())), preferred_element_type=jnp.float32
        ).astype(jnp.bfloat16)

    def scatter_precond(chunk):
        rows_of = pl.ds(chunk * part, part)
        precond[rows_of, :] = jnp.dot(
            lroot_buf[rows_of, :], middle[...], preferred_element_type=jnp.float32
        ).astype(jnp.bfloat16)

        def body(step, carry):
            peer = lax.rem(me + step, n)
            remote(
                precond.at[row_slab(chunk, lax.rem(peer, size)), :], spread[chunk].at[me],
                send_c.at[chunk], recv_c.at[chunk], {"expert": peer},
            ).start()
            return carry

        lax.fori_loop(1, n, body, 0)
        pltpu.make_async_copy(
            precond.at[row_slab(chunk, place), :], spread[chunk].at[me], recv_c.at[chunk]
        ).start()

    def return_blocks(chunk):
        wait_bytes(spread[chunk], recv_c.at[chunk])

        def pick(index):
            for half in range(halves):
                picked[chunk, index, half] = spread[chunk][owner[halves * slot_expert[first + index] + half]]

        def body(step, carry):
            index = lax.rem(place + step, size)
            pick(index)
            remote(
                picked.at[chunk, index], update.at[0, :, row_slab(chunk, place), :],
                send_d.at[chunk], recv_d.at[chunk], {"expert": first + index},
            ).start()
            return carry

        lax.fori_loop(1, size, body, 0)
        pick(place)
        pltpu.make_async_copy(
            picked.at[chunk, place], update.at[0, :, row_slab(chunk, place), :], recv_d.at[chunk]
        ).start()

    for chunk in range(min(AHEAD, chunks)):
        scatter_partials(chunk)
    for load in loads:
        load.start()
    running[size] = jnp.zeros_like(running[size])
    fill_table()
    loads[0].wait()
    for chunk in range(chunks):
        send_sums(chunk)
        if chunk + AHEAD < chunks:
            scatter_partials(chunk + AHEAD)
    for chunk in range(chunks):
        form_grad(chunk)
        if chunk:
            form_middle(chunk - 1)
    form_middle(chunks - 1)
    loads[1].wait()
    for chunk in range(chunks):
        scatter_precond(chunk)

    half_rows = left_buf.shape[0]
    loads[2].wait()
    tile = 128

    def add_left(index, carry):
        rows_of = pl.ds(pl.multiple_of(index * tile, tile), tile)
        product = lax.dot_general(
            grad[pl.ds(pl.multiple_of(core * half_rows + index * tile, tile), tile), :], grad[...],
            (((1,), (1,)), ((), ())), preferred_element_type=jnp.float32,
        )
        left_buf[rows_of, :] = left_buf[rows_of, :] + product / full_cols
        return carry

    lax.fori_loop(0, half_rows // tile, add_left, 0)
    left_store = pltpu.make_async_copy(left_buf, left_next.at[0], store_sem.at[0])
    left_store.start()
    loads[3].wait()

    def add_right(index, carry):
        rows_of = pl.ds(pl.multiple_of(index * tile, tile), tile)
        product = lax.dot_general(
            grad[:, pl.ds(pl.multiple_of(core * cols + index * tile, tile), tile)], grad[...],
            (((0,), (0,)), ((), ())), preferred_element_type=jnp.float32,
        )
        right_buf[rows_of, :] = right_buf[rows_of, :] + product / rows
        return carry

    lax.fori_loop(0, cols // tile, add_right, 0)
    right_store = pltpu.make_async_copy(right_buf, right_next.at[0], store_sem.at[1])
    right_store.start()

    for chunk in range(chunks):
        return_blocks(chunk)
    left_store.wait()
    right_store.wait()
    for chunk in range(chunks):
        wait_bytes(arrived[chunk].at[pl.ds(0, size - 1)], send_a.at[chunk])
        wait_bytes(sums.at[chunk, pl.ds(0, n - 1)], send_b.at[chunk])
        swap(chunk).wait_send()
        wait_bytes(spread[chunk].at[pl.ds(0, n - 1)], send_c.at[chunk])
        wait_bytes(picked.at[chunk, pl.ds(0, size - 1)], send_d.at[chunk])
    for chunk in range(chunks):
        wait_bytes(update.at[0, :, pl.ds(chunk * part, part), :], recv_d.at[chunk])


def on_device(n, partials, counts, slot_expert, owner, left, right, left_root, right_root):
    halves, rows, cols = partials.shape[1:]
    groups = GROUPS
    size = n // groups
    chunks = max(1, min(CHUNKS, rows // (16 * size)))
    sub = rows // chunks // size
    full_cols = right.shape[2]
    anywhere = pl.BlockSpec(memory_space=pl.ANY)
    bf16 = jnp.bfloat16
    dma = pltpu.SemaphoreType.DMA
    scalars = pl.BlockSpec(memory_space=pltpu.SMEM)
    fixed = pl.BlockSpec(memory_space=pltpu.HBM)
    return pl.pallas_call(
        functools.partial(kernel, n, groups, chunks),
        out_shape=(
            jax.ShapeDtypeStruct(partials.shape, bf16),
            jax.ShapeDtypeStruct(left.shape, jnp.float32),
            jax.ShapeDtypeStruct(right.shape, jnp.float32),
        ),
        in_specs=[scalars] * 3 + [fixed] * 5,
        out_specs=(anywhere,) * 3,
        scratch_shapes=[
            pltpu.SMEM((size + 2 * n,), jnp.int32),
            [pltpu.VMEM((size, halves, sub, cols), bf16)] * chunks,
            pltpu.VMEM((size + 1, halves, sub, cols), jnp.float32),
            pltpu.VMEM((chunks, n, sub, cols), bf16),
            pltpu.VMEM((chunks, n, sub, cols), bf16),
            pltpu.VMEM((rows, full_cols), bf16),
            pltpu.VMEM((rows, cols), bf16),
            pltpu.VMEM((rows, cols), bf16),
            [pltpu.VMEM((n, sub, cols), bf16)] * chunks,
            pltpu.VMEM((chunks, size, halves, sub, cols), bf16),
            pltpu.VMEM(left.shape[1:], jnp.float32),
            pltpu.VMEM(right.shape[1:], jnp.float32),
            pltpu.VMEM(left_root.shape[1:], bf16),
            pltpu.VMEM(right_root.shape[1:], bf16),
            dma((4,)),
        ]
        + [dma((chunks,))] * 10
        + [dma((2,))],
        compiler_params=pltpu.CompilerParams(
            collective_id=0, has_side_effects=True, vmem_limit_bytes=60 * 1024 * 1024
        ),
    )(counts, slot_expert, owner, partials, left, right, left_root, right_root)

def solution(mesh):
    return jax.shard_map(
        functools.partial(on_device, mesh.shape["expert"]),
        mesh=mesh,
        in_specs=(
            P("expert", None, None, "mp"),
            P(),
            P(),
            P(),
            P("expert", "mp", None),
            P("expert", "mp", None),
            P("expert", None, None),
            P("expert", "mp", None),
        ),
        out_specs=(P("expert", None, None, "mp"), P("expert", "mp", None), P("expert", "mp", None)),
        check_vma=False,
    )
```

```python
import functools

import jax
import jax.numpy as jnp
from jax import lax
from jax.experimental import pallas as pl
from jax.experimental.pallas import tpu as pltpu
from jax.sharding import PartitionSpec as P

GROUPS = 2
CHUNKS = 4
AHEAD = 3
PIECES = 2


def kernel(
    n, groups, chunks, counts, slot_expert, owner, partials, left, right, left_root, right_root,
    update, left_next, right_next,
    table, arrived, running, sums, blocks, grad, middle, precond, spread, picked,
    left_buf, right_buf, lroot_buf, rroot_buf,
    load_sem, send_a, recv_a, send_b, recv_b, send_p, recv_p, send_c, recv_c, send_d, recv_d, store_sem,
):
    size = n // groups
    halves, rows, cols = partials.shape[1:]
    part = rows // chunks
    sub = part // size
    full_cols = grad.shape[1]
    me = lax.axis_index("expert")
    core = lax.axis_index("mp")
    first = me // size * size
    place = lax.rem(me, size)
    source_at, half_at = size, size + n

    def remote(src, dst, send, recv, peer):
        return pltpu.make_async_remote_copy(
            src_ref=src, dst_ref=dst, send_sem=send, recv_sem=recv,
            device_id=peer, device_id_type=pl.DeviceIdType.MESH,
        )

    def wait_bytes(ref, sem):
        pltpu.make_async_copy(ref, ref, sem).wait()

    def row_slab(chunk, index):
        return pl.ds(pl.multiple_of(chunk * part + index * sub, sub), sub)

    my_cols = pl.ds(pl.multiple_of(core * cols, 128), cols)

    loads = [
        pltpu.make_async_copy(right_root.at[0], rroot_buf, load_sem.at[0]),
        pltpu.make_async_copy(left_root.at[0], lroot_buf, load_sem.at[1]),
        pltpu.make_async_copy(left.at[0], left_buf, load_sem.at[2]),
        pltpu.make_async_copy(right.at[0], right_buf, load_sem.at[3]),
    ]

    barrier = pltpu.get_barrier_semaphore()

    def greet(step, carry):
        pl.semaphore_signal(
            barrier, inc=1, device_id={"expert": lax.rem(me + step, n)},
            device_id_type=pl.DeviceIdType.MESH,
        )
        return carry

    lax.fori_loop(1, n, greet, 0)
    pl.semaphore_signal(barrier, inc=1, device_id={"mp": 1 - core}, device_id_type=pl.DeviceIdType.MESH)
    pl.semaphore_wait(barrier, n)

    def scatter_partials(chunk):
        def body(step, carry):
            index = lax.rem(place + step, size)
            remote(
                partials.at[0, :, row_slab(chunk, index), :],
                arrived[chunk].at[place], send_a.at[chunk], recv_a.at[chunk],
                {"expert": first + index},
            ).start()
            return carry

        lax.fori_loop(1, size, body, 0)
        pltpu.make_async_copy(
            partials.at[0, :, row_slab(chunk, place), :], arrived[chunk].at[place], recv_a.at[chunk]
        ).start()

    def block_at(device):
        return lax.fori_loop(
            0, n, lambda block, found: jnp.where(owner[block] == device, block, found), jnp.int32(0), unroll=8
        )

    def fill_table():
        def link(index, carry):
            expert = slot_expert[first + index]
            table[index] = lax.fori_loop(
                0, size,
                lambda other, found: jnp.where(
                    (slot_expert[first + other] == expert) & (other < index), other, found
                ),
                jnp.int32(size), unroll=8,
            )
            return carry

        lax.fori_loop(0, size, link, 0)

        def locate(device, carry):
            block = block_at(device)
            expert = block // halves
            table[source_at + device] = lax.fori_loop(
                0, size,
                lambda other, found: jnp.where(slot_expert[first + other] == expert, other, found),
                jnp.int32(size), unroll=8,
            )
            table[half_at + device] = block - expert * halves
            return carry

        lax.fori_loop(0, n, locate, 0)

    def half_sum(device):
        return running[table[source_at + device], table[half_at + device]].astype(jnp.bfloat16)

    def send_sums(chunk):
        wait_bytes(arrived[chunk], recv_a.at[chunk])
        for half in range(halves):
            def add(index, carry):
                running[index, half] = running[table[index], half] + arrived[chunk][index, half].astype(jnp.float32)
                return carry

            lax.fori_loop(0, size, add, 0)

        def send(step, carry):
            peer = lax.rem(me + step, n)
            sums[chunk, peer] = half_sum(peer)
            remote(
                sums.at[chunk, peer], blocks.at[chunk, me], send_b.at[chunk], recv_b.at[chunk],
                {"expert": peer},
            ).start()
            return carry

        lax.fori_loop(1, n, send, 0)
        sums[chunk, me] = half_sum(me)
        pltpu.make_async_copy(sums.at[chunk, me], blocks.at[chunk, me], recv_b.at[chunk]).start()

    def form_grad(chunk):
        wait_bytes(blocks.at[chunk], recv_b.at[chunk])
        count = counts[block_at(me) // halves].astype(jnp.float32)

        def form(index, carry):
            total = blocks[chunk, index].astype(jnp.float32)
            for group in range(1, groups):
                total = total + blocks[chunk, group * size + index].astype(jnp.float32)
            grad[row_slab(chunk, index), my_cols] = (total / count).astype(jnp.bfloat16)
            return carry

        lax.fori_loop(0, size, form, 0)
        swap(chunk).start()

    def swap(chunk):
        rows_of = pl.ds(chunk * part, part)
        return remote(
            grad.at[rows_of, my_cols], grad.at[rows_of, my_cols],
            send_p.at[chunk], recv_p.at[chunk], {"mp": 1 - core},
        )

    def form_middle(chunk):
        rows_of = pl.ds(chunk * part, part)
        swap(chunk).wait_recv()
        middle[rows_of, :] = lax.dot_general(
            grad[rows_of, :], rroot_buf[...], (((1,), (1,)), ((), ())), preferred_element_type=jnp.float32
        ).astype(jnp.bfloat16)

    def scatter_precond(chunk):
        rows_of = pl.ds(chunk * part, part)
        precond[rows_of, :] = jnp.dot(
            lroot_buf[rows_of, :], middle[...], preferred_element_type=jnp.float32
        ).astype(jnp.bfloat16)

        def body(step, carry):
            peer = lax.rem(me + step, n)
            remote(
                precond.at[row_slab(chunk, lax.rem(peer, size)), :], spread[chunk].at[me],
                send_c.at[chunk], recv_c.at[chunk], {"expert": peer},
            ).start()
            return carry

        lax.fori_loop(1, n, body, 0)
        pltpu.make_async_copy(
            precond.at[row_slab(chunk, place), :], spread[chunk].at[me], recv_c.at[chunk]
        ).start()

    def return_blocks(chunk):
        wait_bytes(spread[chunk], recv_c.at[chunk])

        def pick(index):
            for half in range(halves):
                picked[chunk, index, half] = spread[chunk][owner[halves * slot_expert[first + index] + half]]

        def body(step, carry):
            index = lax.rem(place + step, size)
            pick(index)
            remote(
                picked.at[chunk, index], update.at[0, :, row_slab(chunk, place), :],
                send_d.at[chunk], recv_d.at[chunk], {"expert": first + index},
            ).start()
            return carry

        lax.fori_loop(1, size, body, 0)
        pick(place)
        pltpu.make_async_copy(
            picked.at[chunk, place], update.at[0, :, row_slab(chunk, place), :], recv_d.at[chunk]
        ).start()

    for chunk in range(min(AHEAD, chunks)):
        scatter_partials(chunk)
    for load in loads:
        load.start()
    running[size] = jnp.zeros_like(running[size])
    fill_table()
    loads[0].wait()
    for chunk in range(chunks):
        send_sums(chunk)
        if chunk + AHEAD < chunks:
            scatter_partials(chunk + AHEAD)
    for chunk in range(chunks):
        form_grad(chunk)
        if chunk:
            form_middle(chunk - 1)
    form_middle(chunks - 1)
    loads[1].wait()
    for chunk in range(chunks):
        scatter_precond(chunk)

    half_rows = left_buf.shape[0]
    loads[2].wait()
    tile = 128

    def add_left(index, carry):
        rows_of = pl.ds(pl.multiple_of(index * tile, tile), tile)
        product = lax.dot_general(
            grad[pl.ds(pl.multiple_of(core * half_rows + index * tile, tile), tile), :], grad[...],
            (((1,), (1,)), ((), ())), preferred_element_type=jnp.float32,
        )
        left_buf[rows_of, :] = left_buf[rows_of, :] + product / full_cols
        return carry

    lax.fori_loop(0, half_rows // tile, add_left, 0)
    left_store = pltpu.make_async_copy(left_buf, left_next.at[0], store_sem.at[0])
    left_store.start()
    loads[3].wait()

    def add_right(index, carry):
        rows_of = pl.ds(pl.multiple_of(index * tile, tile), tile)
        product = lax.dot_general(
            grad[:, pl.ds(pl.multiple_of(core * cols + index * tile, tile), tile)], grad[...],
            (((0,), (0,)), ((), ())), preferred_element_type=jnp.float32,
        )
        right_buf[rows_of, :] = right_buf[rows_of, :] + product / rows
        return carry

    lax.fori_loop(0, cols // tile, add_right, 0)
    right_store = pltpu.make_async_copy(right_buf, right_next.at[0], store_sem.at[1])
    right_store.start()

    for chunk in range(chunks):
        return_blocks(chunk)
    left_store.wait()
    right_store.wait()
    for chunk in range(chunks):
        wait_bytes(arrived[chunk].at[pl.ds(0, size - 1)], send_a.at[chunk])
        wait_bytes(sums.at[chunk, pl.ds(0, n - 1)], send_b.at[chunk])
        swap(chunk).wait_send()
        wait_bytes(spread[chunk].at[pl.ds(0, n - 1)], send_c.at[chunk])
        wait_bytes(picked.at[chunk, pl.ds(0, size - 1)], send_d.at[chunk])
    for chunk in range(chunks):
        wait_bytes(update.at[0, :, pl.ds(chunk * part, part), :], recv_d.at[chunk])


def store_kernel(*refs):
    count = len(refs) // 3
    sources, targets, buffers = refs[:count], refs[count : 2 * count], refs[2 * count : 3 * count]
    load_sem, store_sem = refs[3 * count :]
    loads, stores = [], []
    for source, target, buffer in zip(sources, targets, buffers):
        rows = source.shape[-2] // PIECES
        for lead in range(source.shape[1] if len(source.shape) == 4 else 1):
            for piece in range(PIECES):
                at = pl.ds(piece * rows, rows)
                at = (0, lead, at) if len(source.shape) == 4 else (0, at)
                index = len(loads)
                loads.append(pltpu.make_async_copy(source.at[at], buffer.at[at], load_sem.at[index]))
                stores.append(pltpu.make_async_copy(buffer.at[at], target.at[at], store_sem.at[index]))
    for load in loads:
        load.start()
    for load, store in zip(loads, stores):
        load.wait()
        store.start()
    for store in stores:
        store.wait()


def on_device(n, partials, counts, slot_expert, owner, left, right, left_root, right_root):
    halves, rows, cols = partials.shape[1:]
    groups = GROUPS
    size = n // groups
    chunks = max(1, min(CHUNKS, rows // (16 * size)))
    sub = rows // chunks // size
    full_cols = right.shape[2]
    anywhere = pl.BlockSpec(memory_space=pl.ANY)
    bf16 = jnp.bfloat16
    dma = pltpu.SemaphoreType.DMA
    scalars = pl.BlockSpec(memory_space=pltpu.SMEM)
    fixed = pl.BlockSpec(memory_space=pltpu.HBM)
    results = pl.pallas_call(
        functools.partial(kernel, n, groups, chunks),
        out_shape=(
            jax.ShapeDtypeStruct(partials.shape, bf16),
            jax.ShapeDtypeStruct(left.shape, jnp.float32),
            jax.ShapeDtypeStruct(right.shape, jnp.float32),
        ),
        in_specs=[scalars] * 3 + [fixed] * 5,
        out_specs=(anywhere,) * 3,
        scratch_shapes=[
            pltpu.SMEM((size + 2 * n,), jnp.int32),
            [pltpu.VMEM((size, halves, sub, cols), bf16)] * chunks,
            pltpu.VMEM((size + 1, halves, sub, cols), jnp.float32),
            pltpu.VMEM((chunks, n, sub, cols), bf16),
            pltpu.VMEM((chunks, n, sub, cols), bf16),
            pltpu.VMEM((rows, full_cols), bf16),
            pltpu.VMEM((rows, cols), bf16),
            pltpu.VMEM((rows, cols), bf16),
            [pltpu.VMEM((n, sub, cols), bf16)] * chunks,
            pltpu.VMEM((chunks, size, halves, sub, cols), bf16),
            pltpu.VMEM(left.shape[1:], jnp.float32),
            pltpu.VMEM(right.shape[1:], jnp.float32),
            pltpu.VMEM(left_root.shape[1:], bf16),
            pltpu.VMEM(right_root.shape[1:], bf16),
            dma((4,)),
        ]
        + [dma((chunks,))] * 10
        + [dma((2,))],
        compiler_params=pltpu.CompilerParams(
            collective_id=0, has_side_effects=True, vmem_limit_bytes=60 * 1024 * 1024
        ),
    )(counts, slot_expert, owner, partials, left, right, left_root, right_root)
    copies = PIECES * (halves + 2)
    return pl.pallas_call(
        store_kernel,
        out_shape=tuple(jax.ShapeDtypeStruct(result.shape, result.dtype) for result in results),
        in_specs=[anywhere] * 3,
        out_specs=(anywhere,) * 3,
        scratch_shapes=[pltpu.VMEM(result.shape, result.dtype) for result in results]
        + [dma((copies,)), dma((copies,))],
        compiler_params=pltpu.CompilerParams(vmem_limit_bytes=60 * 1024 * 1024),
    )(*results)

def solution(mesh):
    return jax.shard_map(
        functools.partial(on_device, mesh.shape["expert"]),
        mesh=mesh,
        in_specs=(
            P("expert", None, None, "mp"),
            P(),
            P(),
            P(),
            P("expert", "mp", None),
            P("expert", "mp", None),
            P("expert", None, None),
            P("expert", "mp", None),
        ),
        out_specs=(P("expert", None, None, "mp"), P("expert", "mp", None), P("expert", "mp", None)),
        check_vma=False,
    )
```

```python
import functools

import jax
import jax.numpy as jnp
from jax import lax
from jax.experimental import pallas as pl
from jax.experimental.pallas import tpu as pltpu
from jax.sharding import PartitionSpec as P

GROUPS = 2
CHUNKS = 4
AHEAD = 3
PIECES = 1


def kernel(
    n, groups, chunks, counts, slot_expert, owner, partials, left, right, left_root, right_root,
    update, left_next, right_next,
    table, arrived, running, sums, blocks, grad, middle, precond, spread, picked,
    left_buf, right_buf, lroot_buf, rroot_buf,
    load_sem, send_a, recv_a, send_b, recv_b, send_p, recv_p, send_c, recv_c, send_d, recv_d, store_sem,
):
    size = n // groups
    halves, rows, cols = partials.shape[1:]
    part = rows // chunks
    sub = part // size
    full_cols = grad.shape[1]
    me = lax.axis_index("expert")
    core = lax.axis_index("mp")
    first = me // size * size
    place = lax.rem(me, size)
    source_at, half_at = size, size + n

    def remote(src, dst, send, recv, peer):
        return pltpu.make_async_remote_copy(
            src_ref=src, dst_ref=dst, send_sem=send, recv_sem=recv,
            device_id=peer, device_id_type=pl.DeviceIdType.MESH,
        )

    def wait_bytes(ref, sem):
        pltpu.make_async_copy(ref, ref, sem).wait()

    def row_slab(chunk, index):
        return pl.ds(pl.multiple_of(chunk * part + index * sub, sub), sub)

    my_cols = pl.ds(pl.multiple_of(core * cols, 128), cols)

    loads = [
        pltpu.make_async_copy(right_root.at[0], rroot_buf, load_sem.at[0]),
        pltpu.make_async_copy(left_root.at[0], lroot_buf, load_sem.at[1]),
        pltpu.make_async_copy(left.at[0], left_buf, load_sem.at[2]),
        pltpu.make_async_copy(right.at[0], right_buf, load_sem.at[3]),
    ]

    barrier = pltpu.get_barrier_semaphore()

    def greet(step, carry):
        pl.semaphore_signal(
            barrier, inc=1, device_id={"expert": lax.rem(me + step, n)},
            device_id_type=pl.DeviceIdType.MESH,
        )
        return carry

    lax.fori_loop(1, n, greet, 0)
    pl.semaphore_signal(barrier, inc=1, device_id={"mp": 1 - core}, device_id_type=pl.DeviceIdType.MESH)
    for load in loads:
        load.start()
    running[size] = jnp.zeros_like(running[size])
    pl.semaphore_wait(barrier, n)

    def scatter_partials(chunk):
        def body(step, carry):
            index = lax.rem(place + step, size)
            remote(
                partials.at[0, :, row_slab(chunk, index), :],
                arrived[chunk].at[place], send_a.at[chunk], recv_a.at[chunk],
                {"expert": first + index},
            ).start()
            return carry

        lax.fori_loop(1, size, body, 0)
        pltpu.make_async_copy(
            partials.at[0, :, row_slab(chunk, place), :], arrived[chunk].at[place], recv_a.at[chunk]
        ).start()

    def block_at(device):
        return lax.fori_loop(
            0, n, lambda block, found: jnp.where(owner[block] == device, block, found), jnp.int32(0), unroll=8
        )

    def fill_table():
        def link(index, carry):
            expert = slot_expert[first + index]
            table[index] = lax.fori_loop(
                0, size,
                lambda other, found: jnp.where(
                    (slot_expert[first + other] == expert) & (other < index), other, found
                ),
                jnp.int32(size), unroll=8,
            )
            return carry

        lax.fori_loop(0, size, link, 0)

        def locate(device, carry):
            block = block_at(device)
            expert = block // halves
            table[source_at + device] = lax.fori_loop(
                0, size,
                lambda other, found: jnp.where(slot_expert[first + other] == expert, other, found),
                jnp.int32(size), unroll=8,
            )
            table[half_at + device] = block - expert * halves
            return carry

        lax.fori_loop(0, n, locate, 0)

    def half_sum(device):
        return running[table[source_at + device], table[half_at + device]].astype(jnp.bfloat16)

    def send_sums(chunk):
        wait_bytes(arrived[chunk], recv_a.at[chunk])
        for half in range(halves):
            def add(index, carry):
                running[index, half] = running[table[index], half] + arrived[chunk][index, half].astype(jnp.float32)
                return carry

            lax.fori_loop(0, size, add, 0)

        def send(step, carry):
            peer = lax.rem(me + step, n)
            sums[chunk, peer] = half_sum(peer)
            remote(
                sums.at[chunk, peer], blocks.at[chunk, me], send_b.at[chunk], recv_b.at[chunk],
                {"expert": peer},
            ).start()
            return carry

        lax.fori_loop(1, n, send, 0)
        sums[chunk, me] = half_sum(me)
        pltpu.make_async_copy(sums.at[chunk, me], blocks.at[chunk, me], recv_b.at[chunk]).start()

    def form_grad(chunk):
        wait_bytes(blocks.at[chunk], recv_b.at[chunk])
        count = counts[block_at(me) // halves].astype(jnp.float32)

        def form(index, carry):
            total = blocks[chunk, index].astype(jnp.float32)
            for group in range(1, groups):
                total = total + blocks[chunk, group * size + index].astype(jnp.float32)
            grad[row_slab(chunk, index), my_cols] = (total / count).astype(jnp.bfloat16)
            return carry

        lax.fori_loop(0, size, form, 0)
        swap(chunk).start()

    def swap(chunk):
        rows_of = pl.ds(chunk * part, part)
        return remote(
            grad.at[rows_of, my_cols], grad.at[rows_of, my_cols],
            send_p.at[chunk], recv_p.at[chunk], {"mp": 1 - core},
        )

    def form_middle(chunk):
        rows_of = pl.ds(chunk * part, part)
        swap(chunk).wait_recv()
        middle[rows_of, :] = lax.dot_general(
            grad[rows_of, :], rroot_buf[...], (((1,), (1,)), ((), ())), preferred_element_type=jnp.float32
        ).astype(jnp.bfloat16)

    def scatter_precond(chunk):
        rows_of = pl.ds(chunk * part, part)
        precond[rows_of, :] = jnp.dot(
            lroot_buf[rows_of, :], middle[...], preferred_element_type=jnp.float32
        ).astype(jnp.bfloat16)

        def body(step, carry):
            peer = lax.rem(me + step, n)
            remote(
                precond.at[row_slab(chunk, lax.rem(peer, size)), :], spread[chunk].at[me],
                send_c.at[chunk], recv_c.at[chunk], {"expert": peer},
            ).start()
            return carry

        lax.fori_loop(1, n, body, 0)
        pltpu.make_async_copy(
            precond.at[row_slab(chunk, place), :], spread[chunk].at[me], recv_c.at[chunk]
        ).start()

    def return_blocks(chunk):
        wait_bytes(spread[chunk], recv_c.at[chunk])

        def pick(index):
            for half in range(halves):
                picked[chunk, index, half] = spread[chunk][owner[halves * slot_expert[first + index] + half]]

        def body(step, carry):
            index = lax.rem(place + step, size)
            pick(index)
            remote(
                picked.at[chunk, index], update.at[0, :, row_slab(chunk, place), :],
                send_d.at[chunk], recv_d.at[chunk], {"expert": first + index},
            ).start()
            return carry

        lax.fori_loop(1, size, body, 0)
        pick(place)
        pltpu.make_async_copy(
            picked.at[chunk, place], update.at[0, :, row_slab(chunk, place), :], recv_d.at[chunk]
        ).start()

    for chunk in range(min(AHEAD, chunks)):
        scatter_partials(chunk)
    fill_table()
    loads[0].wait()
    for chunk in range(chunks):
        send_sums(chunk)
        if chunk + AHEAD < chunks:
            scatter_partials(chunk + AHEAD)
    for chunk in range(chunks):
        form_grad(chunk)
        if chunk:
            form_middle(chunk - 1)
    form_middle(chunks - 1)
    loads[1].wait()
    for chunk in range(chunks):
        scatter_precond(chunk)

    half_rows = left_buf.shape[0]
    loads[2].wait()
    tile = 128

    def add_left(index, carry):
        rows_of = pl.ds(pl.multiple_of(index * tile, tile), tile)
        product = lax.dot_general(
            grad[pl.ds(pl.multiple_of(core * half_rows + index * tile, tile), tile), :], grad[...],
            (((1,), (1,)), ((), ())), preferred_element_type=jnp.float32,
        )
        left_buf[rows_of, :] = left_buf[rows_of, :] + product / full_cols
        return carry

    lax.fori_loop(0, half_rows // tile, add_left, 0)
    left_store = pltpu.make_async_copy(left_buf, left_next.at[0], store_sem.at[0])
    left_store.start()
    loads[3].wait()

    def add_right(index, carry):
        rows_of = pl.ds(pl.multiple_of(index * tile, tile), tile)
        product = lax.dot_general(
            grad[:, pl.ds(pl.multiple_of(core * cols + index * tile, tile), tile)], grad[...],
            (((0,), (0,)), ((), ())), preferred_element_type=jnp.float32,
        )
        right_buf[rows_of, :] = right_buf[rows_of, :] + product / rows
        return carry

    lax.fori_loop(0, cols // tile, add_right, 0)
    right_store = pltpu.make_async_copy(right_buf, right_next.at[0], store_sem.at[1])
    right_store.start()

    for chunk in range(chunks):
        return_blocks(chunk)
    left_store.wait()
    right_store.wait()
    for chunk in range(chunks):
        wait_bytes(arrived[chunk].at[pl.ds(0, size - 1)], send_a.at[chunk])
        wait_bytes(sums.at[chunk, pl.ds(0, n - 1)], send_b.at[chunk])
        swap(chunk).wait_send()
        wait_bytes(spread[chunk].at[pl.ds(0, n - 1)], send_c.at[chunk])
        wait_bytes(picked.at[chunk, pl.ds(0, size - 1)], send_d.at[chunk])
    for chunk in range(chunks):
        wait_bytes(update.at[0, :, pl.ds(chunk * part, part), :], recv_d.at[chunk])


def store_kernel(*refs):
    count = len(refs) // 3
    sources, targets, buffers = refs[:count], refs[count : 2 * count], refs[2 * count : 3 * count]
    load_sem, store_sem = refs[3 * count :]
    loads, stores = [], []
    for source, target, buffer in zip(sources, targets, buffers):
        rows = source.shape[-2] // PIECES
        for lead in range(source.shape[1] if len(source.shape) == 4 else 1):
            for piece in range(PIECES):
                at = pl.ds(piece * rows, rows)
                at = (0, lead, at) if len(source.shape) == 4 else (0, at)
                index = len(loads)
                loads.append(pltpu.make_async_copy(source.at[at], buffer.at[at], load_sem.at[index]))
                stores.append(pltpu.make_async_copy(buffer.at[at], target.at[at], store_sem.at[index]))
    for load in loads:
        load.start()
    for load, store in zip(loads, stores):
        load.wait()
        store.start()
    for store in stores:
        store.wait()


def on_device(n, partials, counts, slot_expert, owner, left, right, left_root, right_root):
    halves, rows, cols = partials.shape[1:]
    groups = GROUPS
    size = n // groups
    chunks = max(1, min(CHUNKS, rows // (16 * size)))
    sub = rows // chunks // size
    full_cols = right.shape[2]
    anywhere = pl.BlockSpec(memory_space=pl.ANY)
    bf16 = jnp.bfloat16
    dma = pltpu.SemaphoreType.DMA
    scalars = pl.BlockSpec(memory_space=pltpu.SMEM)
    fixed = pl.BlockSpec(memory_space=pltpu.HBM)
    results = pl.pallas_call(
        functools.partial(kernel, n, groups, chunks),
        out_shape=(
            jax.ShapeDtypeStruct(partials.shape, bf16),
            jax.ShapeDtypeStruct(left.shape, jnp.float32),
            jax.ShapeDtypeStruct(right.shape, jnp.float32),
        ),
        in_specs=[scalars] * 3 + [fixed] * 5,
        out_specs=(anywhere,) * 3,
        scratch_shapes=[
            pltpu.SMEM((size + 2 * n,), jnp.int32),
            [pltpu.VMEM((size, halves, sub, cols), bf16)] * chunks,
            pltpu.VMEM((size + 1, halves, sub, cols), jnp.float32),
            pltpu.VMEM((chunks, n, sub, cols), bf16),
            pltpu.VMEM((chunks, n, sub, cols), bf16),
            pltpu.VMEM((rows, full_cols), bf16),
            pltpu.VMEM((rows, cols), bf16),
            pltpu.VMEM((rows, cols), bf16),
            [pltpu.VMEM((n, sub, cols), bf16)] * chunks,
            pltpu.VMEM((chunks, size, halves, sub, cols), bf16),
            pltpu.VMEM(left.shape[1:], jnp.float32),
            pltpu.VMEM(right.shape[1:], jnp.float32),
            pltpu.VMEM(left_root.shape[1:], bf16),
            pltpu.VMEM(right_root.shape[1:], bf16),
            dma((4,)),
        ]
        + [dma((chunks,))] * 10
        + [dma((2,))],
        compiler_params=pltpu.CompilerParams(
            collective_id=0, has_side_effects=True, vmem_limit_bytes=60 * 1024 * 1024
        ),
    )(counts, slot_expert, owner, partials, left, right, left_root, right_root)
    copies = PIECES * (halves + 2)
    return pl.pallas_call(
        store_kernel,
        out_shape=tuple(jax.ShapeDtypeStruct(result.shape, result.dtype) for result in results),
        in_specs=[anywhere] * 3,
        out_specs=(anywhere,) * 3,
        scratch_shapes=[pltpu.VMEM(result.shape, result.dtype) for result in results]
        + [dma((copies,)), dma((copies,))],
        compiler_params=pltpu.CompilerParams(vmem_limit_bytes=60 * 1024 * 1024),
    )(*results)

def solution(mesh):
    return jax.shard_map(
        functools.partial(on_device, mesh.shape["expert"]),
        mesh=mesh,
        in_specs=(
            P("expert", None, None, "mp"),
            P(),
            P(),
            P(),
            P("expert", "mp", None),
            P("expert", "mp", None),
            P("expert", None, None),
            P("expert", "mp", None),
        ),
        out_specs=(P("expert", None, None, "mp"), P("expert", "mp", None), P("expert", "mp", None)),
        check_vma=False,
    )
```
